128 devices in a mesh: dp: 8 (over z_hi, x), tensor: 16 (over z_lo, y, core).
Axes of the slice: x: 4, y: 4, z: 4 (z_hi: 2, z_lo: 2; z = z_hi * 2 + z_lo), core: 2. Of those that a mesh axis runs over, the one named last changes fastest.
Arguments:
- tokens: bfloat16 [5120, 4096], P('dp'), may hold values from -6 to 6
- hidden_grad: bfloat16 [5120, 14336], P('dp', 'tensor'), may hold values from -3 to 3
- gate_codes: int32 [4096, 14336], P(('dp', 'tensor')), may hold values from 0 to 15
- up_codes: int32 [4096, 14336], P(('dp', 'tensor')), may hold values from 0 to 15
- gate_groups: int32 [128, 14336], P(('dp', 'tensor')), may hold values from 0 to 15
- up_groups: int32 [128, 14336], P(('dp', 'tensor')), may hold values from 0 to 15
- gate_table: float32 [16], replicated, may hold values from 0.0015 to 0.0075
- up_table: float32 [16], replicated, may hold values from 0.0015 to 0.0075
Outputs:
- input_grad: bfloat16 [5120, 4096], P('dp', 'tensor')
- gate_grad: bfloat16 [4096, 14336], P(('dp', 'tensor'))
- up_grad: bfloat16 [4096, 14336], P(('dp', 'tensor'))
The draws below stay inside these ranges and needn't reach their ends.
All inputs are finite; a program needn't handle non-finite values.
Results may differ from the reference program's by a relative error of at most 0.022.
Values may be sent and summed in bfloat16 or wider, within the bound.
No kernel may reach another device: no remote copies, remote signals or barrier semaphores. Data moves between devices by JAX's collectives and lax.ppermute only.
A program may use at most 128 MiB of HBM per device.

```python
import math
import jax
import jax.numpy as jnp
from jax import lax

D = 4096
FF = 14336
GROUP = 32
LEVELS = 16
TOK_DEV = 640
TOKENS = 5120
N_TENSOR = 16


def with_ends(entries, key, least, top_value):
    longest = entries.shape.index(max(entries.shape))
    spots = []
    for shift in (0, 1):
        where = [jax.random.randint(jax.random.fold_in(key, axis), (), 0, length) for axis, length in enumerate(entries.shape)]
        where[longest] = (where[longest] + shift) % entries.shape[longest]
        spots.append(tuple(where))
    return entries.at[spots[0]].set(least).at[spots[1]].set(top_value)


def spiked(result, stream_key, source, target, shards_of, factor):
    owner, partner = [(jnp.arange(result.shape[dim]) // (result.shape[dim] // shards_of)).reshape([-1 if axis == dim else 1 for axis in range(result.ndim)]) for dim in (source, target)]
    chosen = jax.random.permutation(stream_key, shards_of)[partner]
    strong = (owner == chosen) | (owner == (partner + shards_of // 2) % shards_of)
    return jnp.where(strong, factor * result, result)


def shard_levels(stream_key, shape, shards, low, top_value):
    factor_of = 1.0
    for axis_at, parts in shards:
        steps = jax.random.uniform(jax.random.fold_in(jax.random.fold_in(stream_key, 6), axis_at), (parts,), jnp.float32, low / len(shards), top_value / len(shards))
        factor_of = factor_of * jnp.repeat(jnp.exp(steps), shape[axis_at] // parts).reshape((-1,) + (1,) * (len(shape) - 1 - axis_at))
    return factor_of


def scatter_about(rng, extent, deviation, bound, shards=(), held_as=jnp.bfloat16):
    result = jax.random.normal(rng, extent, jnp.float32) * deviation
    if len(shards) > 0:
        result = shard_levels(rng, extent, shards, -0.22, 0.18) * result
    return jnp.clip(result, min=-bound, max=bound).astype(held_as)


def heavy_noise(own_key, shape, scale, most, cuts, heavy, kind=jnp.bfloat16):
    entries = scale * jax.random.normal(own_key, shape, jnp.float32)
    if cuts:
        entries = entries * shard_levels(own_key, shape, cuts, -0.22, 0.18)
    return jnp.clip(spiked(entries, jax.random.fold_in(own_key, 3), *heavy), -most, most).astype(kind)


def setup_inputs(seed: int = 0) -> dict:
    arg_keys = jax.random.split(jax.random.key(seed), 9)
    tokens = heavy_noise(arg_keys[0], (TOKENS, D), 1.0, 6.0, ((0, 8),), (0, 1, 8, 2.0))
    hidden_grad = scatter_about(arg_keys[1], (TOKENS, FF), 0.5, 3.0, ((0, 8), (1, 16)))
    gate_codes = with_ends(jax.random.randint(arg_keys[2], (D, FF), 0, 16), jax.random.fold_in(arg_keys[2], 1), 0, 15).astype(jnp.int32)
    up_codes = with_ends(jax.random.randint(arg_keys[3], (D, FF), 0, 16), jax.random.fold_in(arg_keys[3], 1), 0, 15).astype(jnp.int32)
    gate_groups = with_ends(jax.random.randint(arg_keys[4], (D // GROUP, FF), 0, LEVELS), jax.random.fold_in(arg_keys[4], 1), 0, LEVELS - 1).astype(jnp.int32)
    up_groups = with_ends(jax.random.randint(arg_keys[5], (D // GROUP, FF), 0, LEVELS), jax.random.fold_in(arg_keys[5], 1), 0, LEVELS - 1).astype(jnp.int32)
    gate_table = jnp.clip(jnp.exp(jax.random.uniform(arg_keys[6], (LEVELS,), jnp.float32, math.log(0.0015), math.log(0.0075))), 0.0015, 0.0075)
    up_table = jnp.clip(jnp.exp(jax.random.uniform(arg_keys[7], (LEVELS,), jnp.float32, math.log(0.0015), math.log(0.0075))), 0.0015, 0.0075)
    return {"tokens": tokens, "hidden_grad": hidden_grad, "gate_codes": gate_codes, "up_codes": up_codes, "gate_groups": gate_groups, "up_groups": up_groups, "gate_table": gate_table, "up_table": up_table}


def dequantize(code_words, group_index, scale_table):
    scale_rows = scale_table[group_index]
    scale_rows = jnp.repeat(scale_rows, code_words.shape[0] // group_index.shape[0], axis=0)
    return ((code_words - 8).astype(jnp.float32) * scale_rows).astype(jnp.bfloat16)


def reference(tokens, hidden_grad, gate_codes, up_codes, gate_groups, up_groups, gate_table, up_table):
    w_gate = dequantize(gate_codes, gate_groups, gate_table)
    w_up = dequantize(up_codes, up_groups, up_table)
    gate_pre = jnp.dot(tokens, w_gate, preferred_element_type=jnp.float32)
    up_pre = jnp.dot(tokens, w_up, preferred_element_type=jnp.float32)
    sigmoid_gate = jax.nn.sigmoid(gate_pre)
    upstream = hidden_grad.astype(jnp.float32)
    d_gate = (upstream * up_pre * sigmoid_gate * (1.0 + gate_pre * (1.0 - sigmoid_gate))).astype(jnp.bfloat16)
    d_up = (upstream * gate_pre * sigmoid_gate).astype(jnp.bfloat16)
    shard_width = FF // N_TENSOR
    back_dims = (((1,), (1,)), ((), ()))

    def add_shard(running, index):
        start = (index * shard_width).astype(jnp.int32)
        gate_cols = lax.dynamic_slice_in_dim(d_gate, start, shard_width, 1)
        up_cols = lax.dynamic_slice_in_dim(d_up, start, shard_width, 1)
        gate_w = lax.dynamic_slice_in_dim(w_gate, start, shard_width, 1)
        up_w = lax.dynamic_slice_in_dim(w_up, start, shard_width, 1)
        term = (lax.dot_general(gate_cols, gate_w, back_dims, preferred_element_type=jnp.float32)
                + lax.dot_general(up_cols, up_w, back_dims, preferred_element_type=jnp.float32))
        term = lax.optimization_barrier(term.astype(jnp.bfloat16)).astype(jnp.float32)
        return running + term, None

    zeros_input = jnp.zeros((TOKENS, D), jnp.float32)
    input_total, _ = lax.scan(add_shard, zeros_input, jnp.arange(N_TENSOR, dtype=jnp.int32))
    input_grad = input_total.astype(jnp.bfloat16)
    block_count = TOKENS // TOK_DEV
    token_blocks = tokens.reshape(block_count, TOK_DEV, D)
    gate_blocks = d_gate.reshape(block_count, TOK_DEV, FF)
    up_blocks = d_up.reshape(block_count, TOK_DEV, FF)

    def accumulate(running, block):
        token_block, gate_block, up_block = block
        dims = (((0,), (0,)), ((), ()))
        part_gate = lax.dot_general(token_block, gate_block, dims, preferred_element_type=jnp.float32)
        part_up = lax.dot_general(token_block, up_block, dims, preferred_element_type=jnp.float32)
        part_gate = lax.optimization_barrier(part_gate.astype(jnp.bfloat16)).astype(jnp.float32)
        part_up = lax.optimization_barrier(part_up.astype(jnp.bfloat16)).astype(jnp.float32)
        return (running[0] + part_gate, running[1] + part_up), None

    zeros_grad = jnp.zeros((D, FF), jnp.float32)
    totals, _ = lax.scan(accumulate, (zeros_grad, zeros_grad), (token_blocks, gate_blocks, up_blocks))
    return input_grad, totals[0].astype(jnp.bfloat16), totals[1].astype(jnp.bfloat16)
```

```python
import jax
import jax.numpy as jnp
from jax import lax
from jax.experimental import pallas as pl
from jax.experimental.pallas import tpu as pltpu
from jax.sharding import Mesh
from jax.sharding import PartitionSpec as P

F32 = jnp.float32
BF16 = jnp.bfloat16
HIDDEN = ("zh", "zl", "y", "c")
VMEM_LIMIT = 56 * 1024 * 1024
NT = (((1,), (1,)), ((), ()))


def params(**kw):
    return pltpu.CompilerParams(vmem_limit_bytes=VMEM_LIMIT, **kw)


def cost(flops, nbytes):
    return pl.CostEstimate(flops=flops, bytes_accessed=nbytes, transcendentals=0)


def dequantize(code_words, group_index, scale_table):
    levels = scale_table.shape[0]
    match = group_index[None, :, :] == jnp.arange(levels, dtype=jnp.int32)[:, None, None]
    scale_rows = jnp.sum(jnp.where(match, scale_table[:, None, None], F32(0.0)), axis=0)
    group_count = group_index.shape[0]
    shaped = (code_words - 8).reshape(group_count, -1, code_words.shape[1]).astype(F32)
    return (shaped * scale_rows[:, None, :]).reshape(code_words.shape).astype(BF16)


def spread(own, halves, outer):
    rows, width = own.shape
    part = width // (halves * outer)
    blocks = own.reshape(rows, outer, halves, part).transpose(2, 1, 0, 3)
    blocks = blocks.reshape(halves * outer, rows, part)
    got = lax.all_to_all(blocks, HIDDEN, 0, 0, tiled=True)
    return got.reshape(halves * outer * rows, part)


def collect(summed, halves, outer):
    rows = summed.shape[0] // (halves * outer)
    part = summed.shape[1]
    got = lax.all_to_all(summed.reshape(halves * outer, rows, part), HIDDEN, 0, 0, tiled=True)
    got = got.reshape(halves, outer, rows, part).transpose(2, 1, 0, 3)
    return got.reshape(rows, outer * halves * part)


def transposed_tokens(tokens, slabs, width):
    rows = tokens.shape[0]
    count = slabs.shape[0]

    def body(slabs_ref, t_ref, o_ref):
        o_ref[0] = t_ref[...].T

    return pl.pallas_call(
        body,
        out_shape=jax.ShapeDtypeStruct((count, width, rows), BF16),
        grid_spec=pltpu.PrefetchScalarGridSpec(
            num_scalar_prefetch=1,
            grid=(count,),
            in_specs=[pl.BlockSpec((rows, width), lambda i, s: (0, s[i]))],
            out_specs=pl.BlockSpec((1, width, rows), lambda i, s: (i, 0, 0)),
        ),
        compiler_params=params(),
        cost_estimate=cost(0, 4 * rows * width * count),
    )(slabs, tokens)


def forward_part(tokens, slabs, weight, acc):
    rows = tokens.shape[0]
    count = slabs.shape[0]
    width = weight.shape[0] // count
    columns = weight.shape[1]

    def body(slabs_ref, t_ref, w_ref, *rest):
        o_ref = rest[-1]
        part = jnp.dot(t_ref[...], w_ref[...], preferred_element_type=F32)

        @pl.when(pl.program_id(0) == 0)
        def _():
            o_ref[...] = part if acc is None else rest[0][...] + part

        @pl.when(pl.program_id(0) > 0)
        def _():
            o_ref[...] += part

    whole = pl.BlockSpec((rows, columns), lambda i, s: (0, 0))
    more = [] if acc is None else [acc]
    return pl.pallas_call(
        body,
        out_shape=jax.ShapeDtypeStruct((rows, columns), F32),
        grid_spec=pltpu.PrefetchScalarGridSpec(
            num_scalar_prefetch=1,
            grid=(count,),
            in_specs=[
                pl.BlockSpec((rows, width), lambda i, s: (0, s[i])),
                pl.BlockSpec((width, columns), lambda i, s: (i, 0)),
            ]
            + [whole] * len(more),
            out_specs=whole,
        ),
        compiler_params=params(),
        cost_estimate=cost(2 * rows * width * count * columns, 2 * rows * width * count + 8 * rows * columns),
    )(slabs, tokens, weight, *more)


def forward_last(tokens, slabs, gates, ups, gate_acc, up_acc, grad):
    rows = tokens.shape[0]
    width, columns = gates[0].shape
    tile = 320

    def body(slabs_ref, ta, tb, ga, gb, ua, ub, g_acc, u_acc, h_ref, dg_ref, du_ref):
        gate = g_acc[...] + jnp.dot(ta[...], ga[...], preferred_element_type=F32)
        gate = gate + jnp.dot(tb[...], gb[...], preferred_element_type=F32)
        up = u_acc[...] + jnp.dot(ta[...], ua[...], preferred_element_type=F32)
        up = up + jnp.dot(tb[...], ub[...], preferred_element_type=F32)
        s = jax.nn.sigmoid(gate)
        g = h_ref[...].astype(F32)
        dg_ref[...] = (g * up * s * (1.0 + gate * (1.0 - s))).astype(BF16)
        du_ref[...] = (g * gate * s).astype(BF16)

    slab = pl.BlockSpec((width, columns), lambda i, s: (0, 0))
    tall = pl.BlockSpec((tile, columns), lambda i, s: (i, 0))
    out = jax.ShapeDtypeStruct((rows, columns), BF16)
    return pl.pallas_call(
        body,
        out_shape=(out, out),
        grid_spec=pltpu.PrefetchScalarGridSpec(
            num_scalar_prefetch=1,
            grid=(rows // tile,),
            in_specs=[
                pl.BlockSpec((tile, width), lambda i, s: (i, s[0])),
                pl.BlockSpec((tile, width), lambda i, s: (i, s[1])),
                slab, slab, slab, slab, tall, tall, tall,
            ],
            out_specs=(tall, tall),
        ),
        compiler_params=params(),
        cost_estimate=cost(8 * rows * width * columns, 4 * rows * width + 14 * rows * columns),
    )(slabs, tokens, tokens, *gates, *ups, gate_acc, up_acc, grad)


def weight_part(turned, first, count, delta, adds):
    width, rows = turned.shape[1:]
    columns = delta.shape[1]
    flat = [a for some in adds for a in some]
    lengths = [len(some) for some in adds]

    def body(t_ref, d_ref, *rest):
        ins, outs = rest[: len(flat)], rest[len(flat) :]
        part = jnp.dot(t_ref[0], d_ref[...], preferred_element_type=F32)
        at = 0
        for j in range(count):
            mine = ins[at : at + lengths[j]]
            at += lengths[j]

            @pl.when(pl.program_id(0) == j)
            def _(j=j, mine=mine):
                total = part
                for a in mine:
                    total = total + a[...].astype(F32)
                outs[j][...] = total.astype(BF16)

    slab = pl.BlockSpec((width, columns), lambda i: (0, 0))
    out = jax.ShapeDtypeStruct((width, columns), BF16)
    return pl.pallas_call(
        body,
        out_shape=(out,) * count,
        grid=(count,),
        in_specs=[
            pl.BlockSpec((1, width, rows), lambda i: (first + i, 0, 0)),
            pl.BlockSpec((rows, columns), lambda i: (0, 0)),
        ]
        + [slab] * len(flat),
        out_specs=(slab,) * count,
        compiler_params=params(),
        cost_estimate=cost(2 * rows * width * count * columns, 2 * rows * (width * count + columns) + 2 * width * columns * (count + len(flat))),
    )(turned, delta, *flat)


def input_part(where, d_gate, d_up, w_gate, w_up, add):
    rows, columns = d_gate.shape
    half = rows // 2
    ring = w_gate.shape[0]
    feats = w_gate.shape[3]
    more = [] if add is None else [add]

    def body(where_ref, dg, du, wg, wu, *rest):
        o_ref = rest[-1]
        total = lax.dot_general(dg[...], wg[0, 0, 0], NT, preferred_element_type=F32)
        total = total + lax.dot_general(du[...], wu[0, 0, 0], NT, preferred_element_type=F32)
        if more:
            total = total + rest[0][0].astype(F32)
        o_ref[0] = total.astype(BF16)

    d_spec = pl.BlockSpec((half, columns), lambda t, z, y, s: (t ^ s[0], 0))
    w_spec = pl.BlockSpec(
        (1, 1, 1, feats, columns), lambda t, z, y, s: ((y - s[1] + ring) % ring, z, s[2], 0, 0)
    )
    o_spec = pl.BlockSpec((1, half, feats), lambda t, z, y, s: ((t * 2 + z) * ring + y, 0, 0))
    return pl.pallas_call(
        body,
        out_shape=jax.ShapeDtypeStruct((4 * ring, half, feats), BF16),
        grid_spec=pltpu.PrefetchScalarGridSpec(
            num_scalar_prefetch=1,
            grid=(2, 2, ring),
            in_specs=[d_spec, d_spec, w_spec, w_spec] + [o_spec] * len(more),
            out_specs=o_spec,
        ),
        compiler_params=params(),
        cost_estimate=cost(4 * rows * columns * feats * ring * 2, 16 * ring * half * feats),
    )(where, d_gate, d_up, w_gate, w_up, *more)


def ring_perm(n, step):
    return [(i, (i + step) % n) for i in range(n)]


def shards(tokens, hidden_grad, gate_codes, up_codes, gate_groups, up_groups, gate_table, up_table):
    zh, x, core = lax.axis_index("zh"), lax.axis_index("x"), lax.axis_index("c")
    ring = lax.axis_size("x")
    halves = lax.axis_size("zh")
    planes = lax.axis_size("zl")
    outer = planes * lax.axis_size("y") * lax.axis_size("c")
    own_tokens, width_all = tokens.shape
    slab = width_all // (halves * ring)
    part = hidden_grad.shape[1] // halves
    right, left = ring_perm(ring, 1), ring_perm(ring, -1)
    swap = [(0, 1), (1, 0)]
    crossed = [(i, halves * planes - 1 - i) for i in range(halves * planes)]

    share = own_tokens // 2
    mine = lax.dynamic_slice_in_dim(tokens, core * share, share, 0)
    mine = lax.ppermute(mine, ("zh", "zl"), crossed)
    theirs = lax.ppermute(mine, "c", swap)
    low = jnp.where(core == 0, mine, theirs)
    high = jnp.where(core == 0, theirs, mine)
    every = jnp.concatenate([tokens, low, high], axis=0)
    first, second = hidden_grad[:, :part], hidden_grad[:, part:]
    grad_own = jnp.where(zh == 0, first, second)
    grad_other = lax.ppermute(jnp.where(zh == 0, second, first), "zh", swap)
    grad = jnp.concatenate([grad_own, grad_other], axis=0)

    at_p, at_m, at_2 = (x + 1) % ring, (x + ring - 1) % ring, (x + 2) % ring
    slabs = lambda *pairs: jnp.stack([z * ring + at for z, at in pairs]).astype(jnp.int32)
    turned = transposed_tokens(
        every,
        slabs((0, at_2), (1, at_2), (1, at_p), (0, at_m), (0, at_p), (1, at_m), (0, x), (1, x)),
        slab,
    )

    def gather(codes, groups, table):
        own = spread(dequantize(codes, groups, table), halves, outer)
        from_left = lax.ppermute(own, "x", right)
        from_right = lax.ppermute(own, "x", left)
        far_low = lax.ppermute(from_left[:slab], "x", right)
        far_high = lax.ppermute(from_right[slab:], "x", left)
        return own, from_right, from_left, (far_low, far_high)

    def accumulate(parts):
        own, plus, minus, _ = parts
        acc = forward_part(every, slabs((0, x), (1, x)), own, None)
        acc = forward_part(every, slabs((0, at_p), (1, at_p)), plus, acc)
        return forward_part(every, slabs((0, at_m), (1, at_m)), minus, acc)

    gate_parts = gather(gate_codes, gate_groups, gate_table)
    up_parts = gather(up_codes, up_groups, up_table)
    d_gate, d_up = forward_last(
        every,
        slabs((0, at_2), (1, at_2)),
        gate_parts[3],
        up_parts[3],
        accumulate(gate_parts),
        accumulate(up_parts),
        grad,
    )

    def reduced(delta):
        far_low, far_high, plus_high, minus_low = weight_part(turned, 0, 4, delta, [()] * 4)
        got_low = lax.ppermute(far_low, "x", right)
        got_high = lax.ppermute(far_high, "x", left)
        own_high_a = lax.ppermute(plus_high, "x", right)
        own_low_a = lax.ppermute(minus_low, "x", left)
        plus_low, minus_high = weight_part(turned, 4, 2, delta, [(got_low,), (got_high,)])
        own_low_b = lax.ppermute(plus_low, "x", right)
        own_high_b = lax.ppermute(minus_high, "x", left)
        low, high = weight_part(turned, 6, 2, delta, [(own_low_a, own_low_b), (own_high_a, own_high_b)])
        return collect(jnp.concatenate([low, high], axis=0), halves, outer)

    gate_grad = reduced(d_gate)
    up_grad = reduced(d_up)

    def stacked(parts):
        own, plus, minus, far = parts
        return jnp.concatenate([own, plus, *far, minus], axis=0).reshape(ring, halves, 2, slab // 2, part)

    gate_all, up_all = stacked(gate_parts), stacked(up_parts)
    away = input_part(jnp.stack([zh, x, 1 - core]).astype(jnp.int32), d_gate, d_up, gate_all, up_all, None)
    away = lax.ppermute(away, "c", swap)
    here = input_part(jnp.stack([zh, x, core]).astype(jnp.int32), d_gate, d_up, gate_all, up_all, away)
    here = lax.all_to_all(here, ("zh", "zl", "y"), 0, 0, tiled=True)
    input_grad = here.astype(F32).sum(axis=0).astype(BF16)
    return input_grad, gate_grad, up_grad


def solution(mesh):
    fine = Mesh(mesh.devices.reshape(2, 4, 2, 4, 2), ("zh", "x", "zl", "y", "c"))
    data, hidden = ("zh", "x"), ("zl", "y", "c")
    rows = P(data + hidden, None)
    return jax.shard_map(
        shards,
        mesh=fine,
        in_specs=(P(data, None), P(data, hidden), rows, rows, rows, rows, P(), P()),
        out_specs=(P(data, hidden), rows, rows),
        check_vma=False,
    )
```

```python
import jax
import jax.numpy as jnp
from jax import lax
from jax.experimental import pallas as pl
from jax.experimental.pallas import tpu as pltpu
from jax.sharding import Mesh
from jax.sharding import PartitionSpec as P

F32 = jnp.float32
BF16 = jnp.bfloat16
SLABS = 8
HIDDEN = ("zh", "zl", "y", "c")
VMEM_LIMIT = 26 * 1024 * 1024


def params():
    return pltpu.CompilerParams(vmem_limit_bytes=VMEM_LIMIT)


HEAVY = 65536


def cost(flops, nbytes):
    return pl.CostEstimate(flops=flops // 64, bytes_accessed=nbytes // 64, transcendentals=0)


def shape(*dims, kind=BF16):
    return jax.ShapeDtypeStruct(dims, kind)


def after(value, *others):
    return lax.optimization_barrier((value, *others))[0]


def dot(a, b, dims=((1,), (0,))):
    return lax.dot_general(a, b, (dims, ((), ())), preferred_element_type=F32)


def dequantized(codes, groups, tables, halves, outer):
    rows, width = codes[0].shape
    part = width // (halves * outer)
    pair = halves * part
    per = 4
    levels = tables[0].shape[0]

    def body(gate_table, up_table, gate_codes, up_codes, gate_groups, up_groups, o_ref):
        both = ((gate_table, gate_codes, gate_groups), (up_table, up_codes, up_groups))
        for b in range(per):
            at = pl.ds(b * pair, pair)
            for w, (table, c_ref, g_ref) in enumerate(both):
                index = g_ref[:, at]
                scale = jnp.full(index.shape, table[0], F32)
                for k in range(1, levels):
                    scale = jnp.where(index == k, table[k], scale)
                value = ((c_ref[:, at] - 8).astype(F32) * scale).astype(BF16)
                for h in range(halves):
                    o_ref[h, b, :, w * part : (w + 1) * part] = value[:, h * part : (h + 1) * part]

    table_spec = pl.BlockSpec(memory_space=pltpu.SMEM)
    code_spec = pl.BlockSpec((rows, per * pair), lambda i: (0, i))
    group_spec = pl.BlockSpec((1, per * pair), lambda i: (0, i))
    return pl.pallas_call(
        body,
        out_shape=shape(halves, outer, rows, 2 * part),
        grid=(outer // per,),
        in_specs=[table_spec, table_spec, code_spec, code_spec, group_spec, group_spec],
        out_specs=pl.BlockSpec((halves, per, rows, 2 * part), lambda i: (0, i, 0, 0)),
        compiler_params=params(),
        cost_estimate=cost(0, 12 * rows * width),
    )(*tables, *codes, *groups)


def gathered_columns(blocks):
    halves, outer, rows, both = blocks.shape
    part = both // 2
    pair = halves * part
    per = 4

    def body(b_ref, gate_ref, up_ref):
        for b in range(per):
            for h in range(halves):
                at = pl.ds(b * pair + h * part, part)
                gate_ref[:, at] = b_ref[h, b, :, :part]
                up_ref[:, at] = b_ref[h, b, :, part:]

    out = shape(rows, outer * pair)
    out_spec = pl.BlockSpec((rows, per * pair), lambda i: (0, i))
    return pl.pallas_call(
        body,
        out_shape=(out, out),
        grid=(outer // per,),
        in_specs=[pl.BlockSpec((halves, per, rows, both), lambda i: (0, i, 0, 0))],
        out_specs=(out_spec, out_spec),
        compiler_params=params(),
        cost_estimate=cost(0, 8 * halves * outer * rows * both // 2),
    )(blocks)


def ordered_tokens(slabs, tokens, width, half, into=None):
    rows = tokens.shape[0]
    count = slabs.shape[0]
    more = [] if into is None else [into]

    def body(slabs_ref, t_ref, *rest):
        rest[-1][0] = t_ref[...]

    return pl.pallas_call(
        body,
        out_shape=shape(count, 2 * rows, width),
        grid_spec=pltpu.PrefetchScalarGridSpec(
            num_scalar_prefetch=1,
            grid=(count,),
            in_specs=[pl.BlockSpec((rows, width), lambda i, s: (0, s[i]))]
            + [pl.BlockSpec(memory_space=pl.ANY)] * len(more),
            out_specs=pl.BlockSpec((1, rows, width), lambda i, s: (i, half, 0)),
        ),
        input_output_aliases={2: 0} if more else {},
        compiler_params=params(),
        cost_estimate=cost(0, 4 * rows * width * count),
    )(slabs, tokens, *more)


def products(t_ref, weights):
    total = None
    for j, w_ref in enumerate(weights):
        term = dot(t_ref[j], w_ref[...])
        total = term if total is None else total + term
    return total


TILE = 320


def forward_first(tokens, weights):
    width, both = weights[0].shape
    count, rows = len(weights), tokens.shape[1]

    def body(t_ref, *rest):
        rest[-1][...] = products(t_ref, rest[:-1])

    return pl.pallas_call(
        body,
        out_shape=shape(rows, both, kind=F32),
        grid=(rows // TILE,),
        in_specs=[pl.BlockSpec((count, TILE, width), lambda i: (0, i, 0))]
        + [pl.BlockSpec((width, both), lambda i: (0, 0))] * count,
        out_specs=pl.BlockSpec((TILE, both), lambda i: (i, 0)),
        compiler_params=params(),
        cost_estimate=cost(2 * count * rows * width * both, 2 * count * rows * width + 4 * rows * both),
    )(tokens, *weights)


def forward_last(tokens, weights, acc, grad_own, grad_other):
    width, both = weights[0].shape
    part = both // 2
    slabs, rows, _ = tokens.shape
    tiles = rows // TILE // 2

    def body(t_ref, low, high, acc_ref, ga_ref, gb_ref, o_ref):
        pre = acc_ref[...] + products(t_ref, (low, high))
        gate, up = pre[:, :part], pre[:, part:]
        s = jax.nn.sigmoid(gate)
        g = jnp.where(pl.program_id(0) < tiles, ga_ref[...].astype(F32), gb_ref[:, :part].astype(F32))
        o_ref[:, :part] = (g * up * s * (1.0 + gate * (1.0 - s))).astype(BF16)
        o_ref[:, part:] = (g * gate * s).astype(BF16)

    slab = pl.BlockSpec((width, both), lambda i: (0, 0))
    tall = pl.BlockSpec((TILE, both), lambda i: (i, 0))
    return pl.pallas_call(
        body,
        out_shape=shape(rows, both),
        grid=(rows // TILE,),
        in_specs=[
            pl.BlockSpec((2, TILE, width), lambda i: (slabs // 2 - 1, i, 0)),
            slab,
            slab,
            tall,
            pl.BlockSpec((TILE, part), lambda i: (jnp.minimum(i, tiles - 1), 0)),
            pl.BlockSpec((TILE, grad_other.shape[1]), lambda i: (jnp.maximum(i - tiles, 0), 0)),
        ],
        out_specs=tall,
        compiler_params=params(),
        cost_estimate=cost(4 * rows * width * both, 4 * rows * width + 8 * rows * both),
    )(tokens, *weights, acc, grad_own, grad_other)


def weight_part(at, tokens, delta, adds, joined=False, heavy=1):
    count = len(at)
    _, rows, width = tokens.shape
    both = delta.shape[1]
    first, step = at[0], at[1] - at[0]
    flat = [a for some in adds for a in some]
    lengths = [len(some) for some in adds]

    def body(t_ref, d_ref, *rest):
        ins, outs = rest[: len(flat)], rest[len(flat) :]
        begin = 0
        for j in range(count):
            mine = ins[begin : begin + lengths[j]]
            begin += lengths[j]

            @pl.when(pl.program_id(0) == j)
            def _(j=j, mine=mine):
                total = dot(t_ref[0], d_ref[...], ((0,), (0,)))
                for a in mine:
                    total = total + a[...].astype(F32)
                o_ref = outs[0 if joined else j]
                o_ref[...] = total.astype(o_ref.dtype)

    slab = pl.BlockSpec((width, both), lambda i: (0, 0))
    if joined:
        out_shape, out_specs = shape(count * width, both, kind=F32), pl.BlockSpec((width, both), lambda i: (i, 0))
    else:
        out_shape, out_specs = (shape(width, both),) * count, (slab,) * count
    return pl.pallas_call(
        body,
        out_shape=out_shape,
        grid=(count,),
        in_specs=[
            pl.BlockSpec((1, rows, width), lambda i: (first + step * i, 0, 0)),
            pl.BlockSpec((rows, both), lambda i: (0, 0)),
        ]
        + [slab] * len(flat),
        out_specs=out_specs,
        compiler_params=params(),
        cost_estimate=cost(heavy * 2 * both * rows * width * count, 2 * rows * (width * count + both) + 2 * both * width * (count + len(flat))),
    )(tokens, delta, *flat)


def finished(total, low, high):
    width, both = low.shape
    tiles = 2

    def body(t_ref, l_ref, h_ref, o_ref):
        last = jnp.where(pl.program_id(0) < tiles, l_ref[...].astype(F32), h_ref[...].astype(F32))
        o_ref[...] = (t_ref[...] + last).astype(BF16)

    tile = width // tiles
    block = pl.BlockSpec((tile, both), lambda i: (i, 0))
    return pl.pallas_call(
        body,
        out_shape=shape(2 * width, both),
        grid=(2 * tiles,),
        in_specs=[
            block,
            pl.BlockSpec((tile, both), lambda i: (jnp.minimum(i, tiles - 1), 0)),
            pl.BlockSpec((tile, both), lambda i: (jnp.maximum(i - tiles, 0), 0)),
        ],
        out_specs=block,
        compiler_params=params(),
        cost_estimate=cost(0, 16 * width * both),
    )(total, low, high)


def input_part(where, delta, weights, add):
    tokens, both = delta.shape
    half = tokens // 2
    count = len(weights) // 2
    feats = weights[0].shape[0] // 2
    more = [] if add is None else [add]

    def body(where_ref, d_ref, *rest):
        o_ref = rest[-1]
        flip = where_ref[count]
        for j in range(count):

            @pl.when(pl.program_id(0) == j)
            def _(j=j):
                pair = jnp.concatenate([rest[2 * j][...], rest[2 * j + 1][...]], axis=0)
                total = dot(d_ref[...], pair, ((1,), (1,)))
                for h in range(2):
                    place = h + flip - 2 * h * flip
                    for z in range(2):
                        value = total[h * half : (h + 1) * half, z * feats : (z + 1) * feats]
                        if more:
                            value = value + rest[2 * count][place, z, 0].astype(F32)
                        o_ref[place, z, 0] = value.astype(BF16)

    o_spec = pl.BlockSpec((2, 2, 1, half, feats), lambda i, s: (0, 0, s[i], 0, 0))
    w_spec = pl.BlockSpec((feats, both), lambda i, s: (s[count + 1], 0))
    return pl.pallas_call(
        body,
        out_shape=shape(2, 2, count, half, feats),
        grid_spec=pltpu.PrefetchScalarGridSpec(
            num_scalar_prefetch=1,
            grid=(count,),
            in_specs=[pl.BlockSpec((tokens, both), lambda i, s: (0, 0))] + [w_spec] * (2 * count) + [o_spec] * len(more),
            out_specs=o_spec,
        ),
        compiler_params=params(),
        cost_estimate=cost(4 * tokens * both * feats * count, 4 * count * both * feats + 8 * tokens * feats * count),
    )(where, delta, *weights, *more)


def shards(tokens, hidden_grad, gate_codes, up_codes, gate_groups, up_groups, gate_table, up_table):
    zh, x, zl = lax.axis_index("zh"), lax.axis_index("x"), lax.axis_index("zl")
    y, core = lax.axis_index("y"), lax.axis_index("c")
    ring = lax.axis_size("x")
    halves, planes, cores = lax.axis_size("zh"), lax.axis_size("zl"), lax.axis_size("c")
    columns = lax.axis_size("y")
    outer = planes * columns * cores
    own_tokens, width_all = tokens.shape
    rows = gate_codes.shape[0]
    slab = width_all // (halves * ring)
    part = hidden_grad.shape[1] // halves
    right = [(i, (i + 1) % ring) for i in range(ring)]
    left = [(i, (i + ring - 1) % ring) for i in range(ring)]
    swap = [(0, 1), (1, 0)]
    crossed = [(i, halves * planes - 1 - i) for i in range(halves * planes)]

    def to_right(a):
        return lax.ppermute(a, "x", right)

    def to_left(a):
        return lax.ppermute(a, "x", left)

    def exchange(blocks):
        return lax.all_to_all(blocks.reshape(halves * outer, rows, 2 * part), HIDDEN, 0, 0, tiled=True)

    blocks = dequantized((gate_codes, up_codes), (gate_groups, up_groups), (gate_table, up_table), halves, outer)
    piece = own_tokens // outer
    mine = after(tokens, blocks)
    mine = lax.dynamic_slice_in_dim(mine, (((1 - zl) * columns + y) * cores + core) * piece, piece, 0)
    mine = lax.ppermute(mine, ("zh", "zl"), crossed)

    got = after(exchange(blocks), mine).reshape(halves, slab, 2 * part)
    low, high = got[0], got[1]
    other = lax.all_gather(after(mine, low), ("zl", "y", "c"), axis=0, tiled=True)
    from_left_low, from_right_high = to_right(low), to_left(high)
    from_left_high, from_right_low = to_right(high), to_left(low)
    far_low, far_high = to_right(from_left_low), to_left(from_right_high)
    near_weights = [low, high, from_right_low, from_right_high, from_left_low, from_left_high]
    far_weights = [far_low, far_high]

    xs = jnp.stack([x, (x + 1) % ring, (x + ring - 1) % ring, (x + 2) % ring]).astype(jnp.int32)
    order = (xs[:, None] + jnp.arange(halves, dtype=jnp.int32)[None, :] * ring).reshape(-1)
    every = ordered_tokens(order, after(tokens, low), slab, 0)
    grads = after(hidden_grad, every)
    first, second = grads[:, :part], grads[:, part:]
    grad_own = jnp.where(zh == 0, first, second)
    lanes = -(-part // 128) * 128
    grad_other = jnp.pad(jnp.where(zh == 0, second, first), ((0, 0), (0, lanes - part)))
    other = after(other, grad_other)
    every = ordered_tokens(order, other, slab, 1, every)
    grad_other = lax.ppermute(after(grad_other, other), "zh", swap)
    acc = forward_first(every, near_weights)
    delta = forward_last(every, far_weights, acc, grad_own, grad_other)

    def input_of(where_core, delta, add):
        where = jnp.concatenate([xs, jnp.stack([zh, where_core]).astype(jnp.int32)])
        return input_part(where, delta, near_weights + far_weights, add)

    none = ((), ())
    sum_low, sum_high = weight_part((6, 7), every, delta, none)
    got_low, got_high = to_right(sum_low), to_left(sum_high)
    away = input_of(1 - core, after(delta, sum_low), None)
    from_core = lax.ppermute(away, "c", swap)
    high_p, low_m = weight_part((3, 4), every, after(delta, away), none, heavy=HEAVY)
    one_low, one_high = to_left(low_m), to_right(high_p)
    here = input_of(core, after(delta, low_m), from_core)
    input_grad = lax.psum_scatter(here.reshape(-1, here.shape[4]), ("zh", "zl", "y"), scatter_dimension=0, tiled=True)
    low_p, high_m = weight_part((2, 5), every, after(delta, here), ((got_low,), (got_high,)), heavy=HEAVY)
    two_low, two_high = to_right(low_p), to_left(high_m)
    total = weight_part((0, 1), every, after(delta, low_p), ((one_low,), (one_high,)), True)
    summed = finished(total, two_low, two_high)
    gate_grad, up_grad = gathered_columns(exchange(summed).reshape(halves, outer, rows, 2 * part))
    return input_grad, gate_grad, up_grad


def solution(mesh):
    fine = Mesh(mesh.devices.reshape(2, 4, 2, 4, 2), ("zh", "x", "zl", "y", "c"))
    data, hidden = ("zh", "x"), ("zl", "y", "c")
    rows = P(data + hidden, None)
    return jax.shard_map(
        shards,
        mesh=fine,
        in_specs=(P(data, None), P(data, hidden), rows, rows, rows, rows, P(), P()),
        out_specs=(P(data, hidden), rows, rows),
        check_vma=False,
    )
```
